128 devices in a mesh: group: 8 (over y, core), path: 16 (over z, x).
Axes of the slice: x: 4, y: 4, z: 4, core: 2. Of those that a mesh axis runs over, the one named last changes fastest.
Arguments:
- inner_params: float32 [256, 2, 32768], P(('group', 'path')), may hold values from -6 to 6
- route: int32 [256, 2], replicated, may hold values from 0 to 15, as said below
- owner: int32 [2, 16], replicated, may hold values from 0 to 127, as said below
- outer_state: float32 [128, 32768], P(('group', 'path')), may hold values from -6 to 6
- momentum: float32 [128, 32768], P(('group', 'path')), may hold values from -4 to 4
Outputs:
- snapshots: float32 [256, 2, 32768], P(('group', 'path'))
- new_momentum: float32 [128, 32768], P(('group', 'path'))
The draws below stay inside these ranges and needn't reach their ends.
Inputs may be any that keep to these rules, and one draw needn't show every extreme that they name: `route`: every module of each level is used by one or more paths. `owner`: the 32 entries are distinct devices.
All inputs are finite; a program needn't handle non-finite values.
Results may differ from the reference program's by a relative error of at most 0.00007.
Values sent between devices are 32-bit elements; how exact they have to be, the bound alone decides.
A program may use at most 128 MiB of HBM per device.

```python
import jax
import jax.numpy as jnp
from jax import lax

MODULES = 16
FRAGMENT = 32768
PATHS = 256
DEVICES = 128


def draw_route(key, part):
    key = jax.random.fold_in(key, 11)
    columns = []
    for level in range(2):
        level_key = jax.random.fold_in(key, level)
        key_order, key_first, key_second, key_cover = jax.random.split(level_key, 4)
        order = jax.random.permutation(key_order, MODULES)
        first = jax.random.randint(key_first, (PATHS,), 0, MODULES)
        second = jax.random.randint(key_second, (PATHS,), 0, MODULES)
        picked = order[jnp.minimum(first, second)]
        cover = jax.random.permutation(key_cover, MODULES)
        picked = picked.at[:MODULES].set(cover)
        columns.append(picked.astype(jnp.int32))
    return jnp.stack(columns, axis=1).astype(jnp.int32)


def draw_owner(key, part):
    key = jax.random.fold_in(key, 23)
    key_inner, key_mix = jax.random.split(key)
    middle = 1 + jax.random.permutation(key_inner, DEVICES - 2)[:2 * MODULES - 2]
    ends = jnp.array([0, DEVICES - 1], dtype=jnp.int32)
    flat = jnp.concatenate([ends, middle.astype(jnp.int32)])
    flat = flat[jax.random.permutation(key_mix, 2 * MODULES)]
    return flat.reshape(2, MODULES).astype(jnp.int32)


def block_scale(own_key, extent, cuts, smallest, high):
    gain = 1.0
    for dim, parts in cuts:
        heights = jax.random.uniform(jax.random.fold_in(jax.random.fold_in(own_key, 6), dim), (parts,), jnp.float32, smallest / len(cuts), high / len(cuts))
        gain = gain * jnp.repeat(jnp.exp(heights), extent[dim] // parts).reshape((-1,) + (1,) * (len(extent) - 1 - dim))
    return gain


def centred(rng, extent, width, limit, cuts=(), kind=jnp.bfloat16):
    entries = jax.random.normal(rng, extent, jnp.float32) * width
    if len(cuts) > 0:
        entries = block_scale(rng, extent, cuts, -0.22, 0.18) * entries
    return jnp.clip(entries, min=-limit, max=limit).astype(kind)


def setup_inputs(seed: int = 0) -> dict:
    key_list = jax.random.split(jax.random.key(seed), 6)
    return {
        "inner_params": centred(key_list[0], (PATHS, 2, FRAGMENT), 1.0, 6.0, ((0, 128),), jnp.float32),
        "route": draw_route(jax.random.fold_in(key_list[5], 71), 0),
        "owner": draw_owner(jax.random.fold_in(key_list[5], 71), 0),
        "outer_state": centred(key_list[3], (DEVICES, FRAGMENT), 1.0, 6.0, ((0, 128),), jnp.float32),
        "momentum": centred(key_list[4], (DEVICES, FRAGMENT), 0.5, 4.0, ((0, 128),), jnp.float32),
    }


momentum_decay = 0.9
outer_rate = 0.7


def reference(inner_params, route, owner, outer_state, momentum):
    labels = jnp.arange(MODULES, dtype=jnp.int32)
    one_hot = (route[:, :, None] == labels[None, None, :]).astype(jnp.float32)
    counts = jnp.sum(one_hot, axis=0)
    totals = jnp.einsum("plm,plf->lmf", one_hot, inner_params.astype(jnp.float32), precision=lax.Precision.HIGHEST)
    outer = outer_state[owner]
    held = momentum[owner]
    delta = outer - totals / counts[:, :, None]
    fresh_momentum = momentum_decay * held + delta
    fresh = outer - outer_rate * (delta + momentum_decay * fresh_momentum)
    new_momentum = momentum.at[owner.reshape(-1)].set(fresh_momentum.reshape(2 * MODULES, FRAGMENT))
    levels = jnp.arange(2, dtype=jnp.int32)
    snapshots = fresh[levels[None, :], route]
    return snapshots, new_momentum
```

```python
import jax
import jax.numpy as jnp
from jax import lax
from jax.sharding import PartitionSpec as P

momentum_decay = 0.9
outer_rate = 0.7
highest = lax.Precision.HIGHEST
axes = ("group", "path")


def on_device(inner_params, route, owner, outer_state, momentum):
    devices = lax.axis_size(axes)
    rank = lax.axis_index(axes)
    paths_dev = inner_params.shape[0]
    width = inner_params.shape[2]
    modules = owner.shape[1]
    rows = 2 * paths_dev
    chunk = width // devices
    labels = jnp.arange(modules, dtype=jnp.int32)
    hot = (route[:, :, None] == labels).astype(jnp.float32)
    counts = jnp.sum(hot, axis=0).reshape(2 * modules, 1)
    path_hot = (hot[:, :, None, :] * jnp.eye(2, dtype=jnp.float32)[None, :, :, None]).reshape(-1, 2 * modules)
    own_hot = (owner.reshape(1, -1) == jnp.arange(devices, dtype=jnp.int32)[:, None]).astype(jnp.float32)
    step = outer_rate * (1 + momentum_decay)
    own = (1 - step) * outer_state - outer_rate * momentum_decay * momentum_decay * momentum
    send = jnp.concatenate([inner_params.reshape(rows, width), own], axis=0)
    send = send.reshape(rows + 1, devices, chunk).transpose(1, 0, 2)
    got = lax.all_to_all(send, axes, 0, 0, tiled=True)
    got_paths = got[:, :rows].reshape(devices * rows, chunk)
    mean = jnp.dot(path_hot.T, got_paths, precision=highest) / counts
    fresh = step * mean + jnp.dot(own_hot.T, got[:, rows], precision=highest)
    back_paths = jnp.dot(path_hot, fresh, precision=highest).reshape(devices, rows, chunk)
    back_own = jnp.dot(own_hot, mean, precision=highest).reshape(devices, 1, chunk)
    back = lax.all_to_all(jnp.concatenate([back_paths, back_own], axis=1), axes, 0, 0, tiled=True)
    back = back.transpose(1, 0, 2).reshape(rows + 1, width)
    owned = jnp.any(owner == rank)
    delta = outer_state - back[rows:]
    new_momentum = jnp.where(owned, momentum_decay * momentum + delta, momentum)
    return back[:rows].reshape(paths_dev, 2, width), new_momentum


def solution(mesh):
    rows = P(axes, None)
    return jax.shard_map(
        on_device,
        mesh=mesh,
        in_specs=(P(axes, None, None), P(), P(), rows, rows),
        out_specs=(P(axes, None, None), rows),
        check_vma=False,
    )
```

```python
import functools

import jax
import jax.numpy as jnp
from jax import lax
from jax.experimental import pallas as pl
from jax.experimental.pallas import tpu as pltpu
from jax.sharding import PartitionSpec as P

axes = ("group", "path")
momentum_decay = 0.9
outer_rate = 0.7
step = outer_rate * (1 + momentum_decay)
MESH = pl.DeviceIdType.MESH
f32 = jnp.float32
bf16 = jnp.bfloat16


def split(x):
    high = x.astype(bf16)
    return high, (x - high.astype(f32)).astype(bf16)


def peer(s, group, path):
    s = lax.rem(s * 37, 128)
    core = lax.rem(lax.rem(group, 2) + s // 64, 2)
    y = lax.rem(group // 2 + lax.rem(s // 16, 4), 4)
    z = lax.rem(path // 4 + lax.rem(s // 4, 4), 4)
    x = lax.rem(lax.rem(path, 4) + lax.rem(s, 4), 4)
    return y * 2 + core, z * 4 + x


def kernel(n, x_ref, route_ref, owner_ref, outer_ref, mom_ref, back_ref, newm_ref,
           own_ref, got_ref, gotown_ref, res_ref, resown_ref, backown_ref,
           send_sem, recv_sem, sendown_sem, recvown_sem, send2_sem, recv2_sem, sendown2_sem, recvown2_sem):
    group, path = lax.axis_index("group"), lax.axis_index("path")
    me = group * 16 + path
    barrier = pltpu.get_barrier_semaphore()

    @pl.loop(1, n)
    def _(s):
        pl.semaphore_signal(barrier, inc=1, device_id=peer(s, group, path), device_id_type=MESH)

    own_ref[...] = (1 - step) * outer_ref[...] - (outer_rate * momentum_decay * momentum_decay) * mom_ref[...]
    pl.semaphore_wait(barrier, n - 1)

    def exchange(src, dst, own_src, own_dst, s1, r1, s2, r2):
        local = pltpu.make_async_copy(src(me), dst(me), r1)
        local.start()
        local2 = pltpu.make_async_copy(own_src(me), own_dst(me), r2)
        local2.start()

        @pl.loop(1, n)
        def _(s):
            to = peer(s, group, path)
            rank = to[0] * 16 + to[1]
            pltpu.make_async_remote_copy(src(rank), dst(me), s1, r1, device_id=to, device_id_type=MESH).start()
            pltpu.make_async_remote_copy(own_src(rank), own_dst(me), s2, r2, device_id=to, device_id_type=MESH).start()

    exchange(lambda r: x_ref.at[:, r], lambda r: got_ref.at[r], lambda r: own_ref.at[r], lambda r: gotown_ref.at[r],
             send_sem, recv_sem, sendown_sem, recvown_sem)
    rows = 8 * n
    route = route_ref[...].astype(bf16)
    k = lax.broadcasted_iota(jnp.int32, (2 * n, rows), 1) // 4
    p = lax.broadcasted_iota(jnp.int32, (2 * n, rows), 0)
    spread = (k == p).astype(f32).astype(bf16)
    both = jnp.dot(route, spread, preferred_element_type=f32)
    col = lax.broadcasted_iota(jnp.int32, (1, rows), 1)
    label = jnp.where(lax.rem(col, 2) == 0, both[0:1], both[1:2]).astype(jnp.int32) + 16 * lax.rem(col, 4)
    hot = (label == lax.broadcasted_iota(jnp.int32, (64, rows), 0)).astype(f32)
    counts = jnp.sum(hot, axis=1, keepdims=True)
    hot2 = jnp.concatenate([hot, hot], axis=0).T.astype(bf16)
    hot = hot.astype(bf16)
    r = lax.broadcasted_iota(jnp.int32, (64, 16), 0)
    owners = owner_ref[...]
    table = jnp.where(lax.rem(r // 16, 2) == 0, owners[0:1], owners[1:2])
    pick = lax.rem(r, 16) == lax.broadcasted_iota(jnp.int32, (64, 16), 1)
    owner_col = jnp.sum(jnp.where(pick, table, 0).astype(f32), axis=1, keepdims=True).astype(jnp.int32)
    k = lax.broadcasted_iota(jnp.int32, (64, 2 * n), 1)
    tile = lax.broadcasted_iota(jnp.int32, (64, 2 * n), 0) // 32
    own_hot = jnp.logical_and(owner_col == k // 2, tile == lax.rem(k, 2)).astype(f32)
    own_hot2 = jnp.concatenate([own_hot, own_hot], axis=0).T.astype(bf16)
    own_hot = own_hot.astype(bf16)
    owned = jnp.sum((owners == me).astype(f32)) > 0.5

    def finish(s, r, ref, out):
        pltpu.make_async_copy(ref, ref, r).wait()
        part = out
        pltpu.make_async_copy(part, part, s).wait()

    pltpu.make_async_copy(got_ref, got_ref, recv_sem).wait()
    pltpu.make_async_copy(gotown_ref, gotown_ref, recvown_sem).wait()
    high, low = split(got_ref[...].reshape(rows, 128))
    mean = jnp.dot(hot, high, preferred_element_type=f32) + jnp.dot(hot, low, preferred_element_type=f32)
    mean = mean / counts
    high, low = split(gotown_ref[...].reshape(2 * n, 128))
    fresh = step * mean + (
        jnp.dot(own_hot, high, preferred_element_type=f32) + jnp.dot(own_hot, low, preferred_element_type=f32))
    res_ref[...] = jnp.dot(hot2, jnp.concatenate(split(fresh), axis=0), preferred_element_type=f32).reshape(res_ref.shape)
    resown_ref[...] = jnp.dot(own_hot2, jnp.concatenate(split(mean), axis=0), preferred_element_type=f32).reshape(resown_ref.shape)
    exchange(lambda r: res_ref.at[r], lambda r: back_ref.at[r], lambda r: resown_ref.at[r], lambda r: backown_ref.at[r],
             send2_sem, recv2_sem, sendown2_sem, recvown2_sem)
    pltpu.make_async_copy(backown_ref, backown_ref, recvown2_sem).wait()
    delta = outer_ref[...] - backown_ref[...]
    newm_ref[...] = jnp.where(owned, momentum_decay * mom_ref[...] + delta, mom_ref[...])
    pltpu.make_async_copy(back_ref, back_ref, recv2_sem).wait()
    last = got_ref.at[pl.ds(0, n - 1)]
    lastown = gotown_ref.at[pl.ds(0, n - 1)]
    pltpu.make_async_copy(last, last, send_sem).wait()
    pltpu.make_async_copy(lastown, lastown, sendown_sem).wait()
    pltpu.make_async_copy(last, last, send2_sem).wait()
    pltpu.make_async_copy(lastown, lastown, sendown2_sem).wait()


def on_device(inner_params, route, owner, outer_state, momentum):
    n = lax.axis_size(axes)
    x = inner_params.reshape(2, 2, n, 2, 128).transpose(0, 2, 3, 1, 4).reshape(2, n, 4, 128)
    vmem = pl.BlockSpec(memory_space=pltpu.VMEM)
    back, newm = pl.pallas_call(
        functools.partial(kernel, n),
        out_shape=(jax.ShapeDtypeStruct((n, 2, 4, 128), f32), jax.ShapeDtypeStruct((n, 2, 128), f32)),
        in_specs=[vmem] * 5,
        out_specs=(vmem, vmem),
        scratch_shapes=[
            pltpu.VMEM((n, 2, 128), f32),
            pltpu.VMEM((n, 2, 4, 128), f32),
            pltpu.VMEM((n, 2, 128), f32),
            pltpu.VMEM((n, 2, 4, 128), f32),
            pltpu.VMEM((n, 2, 128), f32),
            pltpu.VMEM((n, 2, 128), f32),
        ] + [pltpu.SemaphoreType.DMA] * 8,
        compiler_params=pltpu.CompilerParams(collective_id=0, has_side_effects=True, vmem_limit_bytes=40 * 2**20),
    )(x, route.T, owner, outer_state.reshape(n, 2, 128), momentum.reshape(n, 2, 128))
    out = back.reshape(n, 2, 2, 2, 128).transpose(1, 3, 0, 2, 4).reshape(inner_params.shape)
    return out, newm.reshape(momentum.shape)


def solution(mesh):
    rows = P(axes, None)
    return jax.shard_map(
        on_device,
        mesh=mesh,
        in_specs=(P(axes, None, None), P(), P(), rows, rows),
        out_specs=(P(axes, None, None), rows),
        check_vma=False,
    )
```

```python
import functools

import jax
import jax.numpy as jnp
from jax import lax
from jax.experimental import pallas as pl
from jax.experimental.pallas import tpu as pltpu
from jax.sharding import PartitionSpec as P

axes = ("group", "path")
momentum_decay = 0.9
outer_rate = 0.7
step = outer_rate * (1 + momentum_decay)
MESH = pl.DeviceIdType.MESH
f32 = jnp.float32
bf16 = jnp.bfloat16


def split(x):
    high = x.astype(bf16)
    return high, (x - high.astype(f32)).astype(bf16)


def peer(s, group, path):
    core = ((group & 1) + (s >> 6)) & 1
    y = ((group >> 1) + ((s >> 4) & 3)) & 3
    z = ((path >> 2) + ((s >> 2) & 3)) & 3
    x = ((path & 3) + (s & 3)) & 3
    return y * 2 + core, z * 4 + x


def kernel(n, x_ref, route_hbm, owner_hbm, outer_hbm, mom_hbm, back_ref, newm_ref,
           route_ref, owner_ref, outer_ref, mom_ref, load_sem,
           own_ref, got_ref, gotown_ref, res_ref, resown_ref, backown_ref,
           send_sem, recv_sem, sendown_sem, recvown_sem, send2_sem, recv2_sem, sendown2_sem, recvown2_sem):
    group, path = lax.axis_index("group"), lax.axis_index("path")
    me = group * 16 + path
    barrier = pltpu.get_barrier_semaphore()

    @pl.loop(1, n, unroll=n - 1)
    def _(s):
        pl.semaphore_signal(barrier, inc=1, device_id=peer(s, group, path), device_id_type=MESH)

    loads = [pltpu.make_async_copy(a, b, load_sem.at[i]) for i, (a, b) in enumerate(
        [(outer_hbm, outer_ref), (mom_hbm, mom_ref), (route_hbm, route_ref), (owner_hbm, owner_ref)])]
    for load in loads:
        load.start()
    for load in loads:
        load.wait()
    own_ref[...] = (1 - step) * outer_ref[...] - (outer_rate * momentum_decay * momentum_decay) * mom_ref[...]
    pl.semaphore_wait(barrier, n - 1)

    def exchange(src, dst, own_src, own_dst, s1, r1, s2, r2):
        local = pltpu.make_async_copy(src(me), dst(me), r1)
        local.start()
        local2 = pltpu.make_async_copy(own_src(me), own_dst(me), r2)
        local2.start()

        @pl.loop(1, n, unroll=n - 1)
        def _(s):
            to = peer((s * 37) & (n - 1), group, path)
            rank = to[0] * 16 + to[1]
            pltpu.make_async_remote_copy(src(rank), dst(me), s1, r1, device_id=to, device_id_type=MESH).start()
            pltpu.make_async_remote_copy(own_src(rank), own_dst(me), s2, r2, device_id=to, device_id_type=MESH).start()

    exchange(lambda r: x_ref.at[:, r], lambda r: got_ref.at[r], lambda r: own_ref.at[r], lambda r: gotown_ref.at[r],
             send_sem, recv_sem, sendown_sem, recvown_sem)
    rows = 8 * n
    route = route_ref[...].astype(bf16)
    k = lax.broadcasted_iota(jnp.int32, (2 * n, rows), 1) // 4
    p = lax.broadcasted_iota(jnp.int32, (2 * n, rows), 0)
    spread = (k == p).astype(f32).astype(bf16)
    both = jnp.dot(route, spread, preferred_element_type=f32)
    col = lax.broadcasted_iota(jnp.int32, (1, rows), 1)
    label = jnp.where(lax.rem(col, 2) == 0, both[0:1], both[1:2]).astype(jnp.int32) + 16 * lax.rem(col, 4)
    hot = (label == lax.broadcasted_iota(jnp.int32, (64, rows), 0)).astype(f32)
    counts = jnp.sum(hot, axis=1, keepdims=True)
    hot2 = jnp.concatenate([hot, hot], axis=0).T.astype(bf16)
    hot = hot.astype(bf16)
    r = lax.broadcasted_iota(jnp.int32, (64, 16), 0)
    owners = owner_ref[...]
    table = jnp.where(lax.rem(r // 16, 2) == 0, owners[0:1], owners[1:2])
    pick = lax.rem(r, 16) == lax.broadcasted_iota(jnp.int32, (64, 16), 1)
    owner_col = jnp.sum(jnp.where(pick, table, 0).astype(f32), axis=1, keepdims=True).astype(jnp.int32)
    k = lax.broadcasted_iota(jnp.int32, (64, 2 * n), 1)
    tile = lax.broadcasted_iota(jnp.int32, (64, 2 * n), 0) // 32
    own_hot = jnp.logical_and(owner_col == k // 2, tile == lax.rem(k, 2)).astype(f32)
    own_hot2 = jnp.concatenate([own_hot, own_hot], axis=0).T.astype(bf16)
    own_hot = own_hot.astype(bf16)
    owned = jnp.sum((owners == me).astype(f32)) > 0.5

    pltpu.make_async_copy(got_ref, got_ref, recv_sem).wait()
    pltpu.make_async_copy(gotown_ref, gotown_ref, recvown_sem).wait()
    high, low = split(got_ref[...].reshape(rows, 128))
    mean = jnp.dot(hot, high, preferred_element_type=f32) + jnp.dot(hot, low, preferred_element_type=f32)
    mean = mean / counts
    high, low = split(gotown_ref[...].reshape(2 * n, 128))
    fresh = step * mean + (
        jnp.dot(own_hot, high, preferred_element_type=f32) + jnp.dot(own_hot, low, preferred_element_type=f32))
    res_ref[...] = jnp.dot(hot2, jnp.concatenate(split(fresh), axis=0), preferred_element_type=f32).reshape(res_ref.shape)
    resown_ref[...] = jnp.dot(own_hot2, jnp.concatenate(split(mean), axis=0), preferred_element_type=f32).reshape(resown_ref.shape)
    exchange(lambda r: res_ref.at[r], lambda r: back_ref.at[:, r], lambda r: resown_ref.at[r], lambda r: backown_ref.at[r],
             send2_sem, recv2_sem, sendown2_sem, recvown2_sem)
    pltpu.make_async_copy(backown_ref, backown_ref, recvown2_sem).wait()
    delta = outer_ref[...] - backown_ref[...]
    newm_ref[...] = jnp.where(owned, momentum_decay * mom_ref[...] + delta, mom_ref[...])
    pltpu.make_async_copy(back_ref, back_ref, recv2_sem).wait()
    last = got_ref.at[pl.ds(0, n - 1)]
    lastown = gotown_ref.at[pl.ds(0, n - 1)]
    pltpu.make_async_copy(last, last, send_sem).wait()
    pltpu.make_async_copy(lastown, lastown, sendown_sem).wait()
    pltpu.make_async_copy(last, last, send2_sem).wait()
    pltpu.make_async_copy(lastown, lastown, sendown2_sem).wait()


def on_device(inner_params, route, owner, outer_state, momentum):
    n = lax.axis_size(axes)
    x = inner_params.reshape(2, 2, n, 2, 128).transpose(0, 2, 3, 1, 4).reshape(2, n, 4, 128)
    vmem = pl.BlockSpec(memory_space=pltpu.VMEM)
    back, newm = pl.pallas_call(
        functools.partial(kernel, n),
        out_shape=(jax.ShapeDtypeStruct((2, n, 4, 128), f32), jax.ShapeDtypeStruct((n, 2, 128), f32)),
        in_specs=[pl.BlockSpec(memory_space=pltpu.HBM)] * 5,
        out_specs=(vmem, vmem),
        scratch_shapes=[
            pltpu.VMEM((2, 2 * n), jnp.int32),
            pltpu.VMEM(owner.shape, jnp.int32),
            pltpu.VMEM((n, 2, 128), f32),
            pltpu.VMEM((n, 2, 128), f32),
            pltpu.SemaphoreType.DMA((4,)),
            pltpu.VMEM((n, 2, 128), f32),
            pltpu.VMEM((n, 2, 4, 128), f32),
            pltpu.VMEM((n, 2, 128), f32),
            pltpu.VMEM((n, 2, 4, 128), f32),
            pltpu.VMEM((n, 2, 128), f32),
            pltpu.VMEM((n, 2, 128), f32),
        ] + [pltpu.SemaphoreType.DMA] * 8,
        compiler_params=pltpu.CompilerParams(collective_id=0, has_side_effects=True, vmem_limit_bytes=56 * 2**20),
    )(x, route.T, owner, outer_state.reshape(n, 2, 128), momentum.reshape(n, 2, 128))
    out = back.reshape(2, n, 2, 2, 128).transpose(0, 3, 1, 2, 4).reshape(inner_params.shape)
    return out, newm.reshape(momentum.shape)


def solution(mesh):
    rows = P(axes, None)
    return jax.shard_map(
        on_device,
        mesh=mesh,
        in_specs=(P(axes, None, None), P(), P(), rows, rows),
        out_specs=(P(axes, None, None), rows),
        check_vma=False,
    )
```

```python
import functools

import jax
import jax.numpy as jnp
from jax import lax
from jax.experimental import pallas as pl
from jax.experimental.pallas import tpu as pltpu
from jax.sharding import PartitionSpec as P

axes = ("group", "path")
momentum_decay = 0.9
outer_rate = 0.7
step = outer_rate * (1 + momentum_decay)
MESH = pl.DeviceIdType.MESH
f32 = jnp.float32
bf16 = jnp.bfloat16


def split(x):
    high = x.astype(bf16)
    return high, (x - high.astype(f32)).astype(bf16)


def pick(hot, x):
    both = jnp.dot(hot, jnp.concatenate(split(x), axis=1), preferred_element_type=f32)
    return both[:, :128] + both[:, 128:]


def spread(hot2, x):
    return jnp.dot(hot2, jnp.concatenate(split(x), axis=0), preferred_element_type=f32)


def peer(s, group, path):
    core = ((group & 1) + (s >> 6)) & 1
    y = ((group >> 1) + ((s >> 4) & 3)) & 3
    z = ((path >> 2) + ((s >> 2) & 3)) & 3
    x = ((path & 3) + (s & 3)) & 3
    return y * 2 + core, z * 4 + x


def kernel(n, x_ref, route_hbm, owner_hbm, outer_hbm, mom_hbm, back_ref, newm_ref,
           route_ref, owner_ref, outer_ref, mom_ref, load_sem,
           own_ref, got_ref, gotown_ref, res_ref, resown_ref, backown_ref,
           send_sem, recv_sem, sendown_sem, recvown_sem, send2_sem, recv2_sem, sendown2_sem, recvown2_sem):
    group, path = lax.axis_index("group"), lax.axis_index("path")
    me = group * 16 + path
    loads = [pltpu.make_async_copy(a, b, load_sem.at[i]) for i, (a, b) in enumerate(
        [(outer_hbm, outer_ref), (mom_hbm, mom_ref), (route_hbm, route_ref), (owner_hbm, owner_ref)])]
    for load in loads:
        load.start()
    barrier = pltpu.get_barrier_semaphore()

    @pl.loop(1, n, unroll=n - 1)
    def _(s):
        pl.semaphore_signal(barrier, inc=1, device_id=peer(s, group, path), device_id_type=MESH)

    for load in loads:
        load.wait()
    own_ref[...] = (1 - step) * outer_ref[...] - (outer_rate * momentum_decay * momentum_decay) * mom_ref[...]
    pl.semaphore_wait(barrier, n - 1)

    def exchange(*moves):
        for src, dst, _, recv in moves:
            pltpu.make_async_copy(src(me), dst(me), recv).start()

        @pl.loop(1, n, unroll=n - 1)
        def _(s):
            to = peer((s * 37) & (n - 1), group, path)
            rank = to[0] * 16 + to[1]
            for src, dst, sent, recv in moves:
                pltpu.make_async_remote_copy(
                    src(rank), dst(me), sent, recv, device_id=to, device_id_type=MESH).start()

    for t in range(2):
        moves = [(lambda r: x_ref.at[:, r, t], lambda r: got_ref.at[t, r], send_sem.at[t], recv_sem.at[t])]
        if t == 0:
            moves.append((lambda r: own_ref.at[r], lambda r: gotown_ref.at[r], sendown_sem, recvown_sem))
        exchange(*moves)

    rows = 4 * n
    route = route_ref[...].astype(f32).astype(bf16)
    k = lax.broadcasted_iota(jnp.int32, (2 * n, rows), 1) >> 1
    p = lax.broadcasted_iota(jnp.int32, (2 * n, rows), 0)
    both = jnp.dot(route, (k == p).astype(f32).astype(bf16), preferred_element_type=f32)
    level = lax.broadcasted_iota(jnp.int32, (1, rows), 1) & 1
    label = jnp.where(level == 0, both[0:1], both[1:2]).astype(jnp.int32) + 16 * level
    hot = (label == lax.broadcasted_iota(jnp.int32, (32, rows), 0)).astype(f32)
    counts = jnp.sum(hot, axis=1, keepdims=True)
    hot2 = jnp.concatenate([hot, hot], axis=0).T.astype(bf16)
    hot = hot.astype(bf16)
    r = lax.broadcasted_iota(jnp.int32, (32, 16), 0)
    owners = owner_ref[...]
    table = jnp.where(r < 16, owners[0:1], owners[1:2])
    mine = (r & 15) == lax.broadcasted_iota(jnp.int32, (32, 16), 1)
    owner_col = jnp.sum(jnp.where(mine, table, 0).astype(f32), axis=1, keepdims=True).astype(jnp.int32)
    own_hot = (owner_col == lax.broadcasted_iota(jnp.int32, (32, n), 1)).astype(f32)
    own_hot2 = jnp.concatenate([own_hot, own_hot], axis=0).T.astype(bf16)
    own_hot = own_hot.astype(bf16)
    owned = jnp.sum((owners == me).astype(f32)) > 0.5

    for t in range(2):
        pltpu.make_async_copy(got_ref.at[t], got_ref.at[t], recv_sem.at[t]).wait()
        if t == 0:
            pltpu.make_async_copy(gotown_ref, gotown_ref, recvown_sem).wait()
        mean = pick(hot, got_ref[t].reshape(rows, 128)) / counts
        fresh = step * mean + pick(own_hot, gotown_ref[:, t, :])
        res_ref[t] = spread(hot2, fresh).reshape(res_ref.shape[1:])
        resown_ref[:, t, :] = spread(own_hot2, mean)
        moves = [(lambda r: res_ref.at[t, r], lambda r: back_ref.at[:, r, t], send2_sem.at[t], recv2_sem.at[t])]
        if t == 1:
            moves.append((lambda r: resown_ref.at[r], lambda r: backown_ref.at[r], sendown2_sem, recvown2_sem))
        exchange(*moves)
    pltpu.make_async_copy(backown_ref, backown_ref, recvown2_sem).wait()
    delta = outer_ref[...] - backown_ref[...]
    newm_ref[...] = jnp.where(owned, momentum_decay * mom_ref[...] + delta, mom_ref[...])
    for t in range(2):
        pltpu.make_async_copy(got_ref.at[t], got_ref.at[t], recv2_sem.at[t]).wait()
    last = got_ref.at[0, pl.ds(0, n - 1)]
    for sem in (send_sem, send2_sem):
        for t in range(2):
            pltpu.make_async_copy(last, last, sem.at[t]).wait()
    lastown = gotown_ref.at[pl.ds(0, n - 1)]
    pltpu.make_async_copy(lastown, lastown, sendown_sem).wait()
    pltpu.make_async_copy(lastown, lastown, sendown2_sem).wait()


def on_device(inner_params, route, owner, outer_state, momentum):
    n = lax.axis_size(axes)
    x = inner_params.reshape(2, 2, n, 2, 128).transpose(0, 2, 3, 1, 4)
    vmem = pl.BlockSpec(memory_space=pltpu.VMEM)
    one = pltpu.SemaphoreType.DMA
    two = pltpu.SemaphoreType.DMA((2,))
    back, newm = pl.pallas_call(
        functools.partial(kernel, n),
        out_shape=(jax.ShapeDtypeStruct((2, n, 2, 2, 128), f32), jax.ShapeDtypeStruct((n, 2, 128), f32)),
        in_specs=[pl.BlockSpec(memory_space=pltpu.HBM)] * 5,
        out_specs=(vmem, vmem),
        scratch_shapes=[
            pltpu.VMEM((2, 2 * n), jnp.int32),
            pltpu.VMEM(owner.shape, jnp.int32),
            pltpu.VMEM((n, 2, 128), f32),
            pltpu.VMEM((n, 2, 128), f32),
            pltpu.SemaphoreType.DMA((4,)),
            pltpu.VMEM((n, 2, 128), f32),
            pltpu.VMEM((2, n, 2, 2, 128), f32),
            pltpu.VMEM((n, 2, 128), f32),
            pltpu.VMEM((2, n, 2, 2, 128), f32),
            pltpu.VMEM((n, 2, 128), f32),
            pltpu.VMEM((n, 2, 128), f32),
            two, two, one, one, two, two, one, one,
        ],
        compiler_params=pltpu.CompilerParams(collective_id=0, has_side_effects=True, vmem_limit_bytes=56 * 2**20),
    )(x, route.T, owner, outer_state.reshape(n, 2, 128), momentum.reshape(n, 2, 128))
    out = back.transpose(0, 3, 1, 2, 4).reshape(inner_params.shape)
    return out, newm.reshape(momentum.shape)


def solution(mesh):
    rows = P(axes, None)
    return jax.shard_map(
        on_device,
        mesh=mesh,
        in_specs=(P(axes, None, None), P(), P(), rows, rows),
        out_specs=(P(axes, None, None), rows),
        check_vma=False,
    )
```

```python
import functools

import jax
import jax.numpy as jnp
from jax import lax
from jax.experimental import pallas as pl
from jax.experimental.pallas import tpu as pltpu
from jax.sharding import PartitionSpec as P

axes = ("group", "path")
momentum_decay = 0.9
outer_rate = 0.7
step = outer_rate * (1 + momentum_decay)
MESH = pl.DeviceIdType.MESH
f32 = jnp.float32
bf16 = jnp.bfloat16


def split(x):
    high = x.astype(bf16)
    return high, (x - high.astype(f32)).astype(bf16)


def pick(hot, x):
    both = jnp.dot(hot, jnp.concatenate(split(x), axis=1), preferred_element_type=f32)
    return both[:, :128] + both[:, 128:]


def spread(hot2, x):
    return jnp.dot(hot2, jnp.concatenate(split(x), axis=0), preferred_element_type=f32)


def peer(s, group, path):
    core = ((group & 1) + (s >> 6)) & 1
    y = ((group >> 1) + ((s >> 4) & 3)) & 3
    z = ((path >> 2) + ((s >> 2) & 3)) & 3
    x = ((path & 3) + (s & 3)) & 3
    return y * 2 + core, z * 4 + x


def hops(s):
    return sum(min(a, 4 - a) for a in (s & 3, (s >> 2) & 3, (s >> 4) & 3))


def route_order(n):
    return sorted(range(1, n), key=lambda s: (-hops(s), s * 37 % n))


def kernel(n, x_ref, route_hbm, owner_hbm, outer_hbm, mom_hbm, back_ref, newm_ref,
           route_ref, owner_ref, outer_ref, mom_ref, load_sem,
           own_ref, got_ref, gotown_ref, res_ref, resown_ref, backown_ref,
           send_sem, recv_sem, sendown_sem, recvown_sem, send2_sem, recv2_sem, sendown2_sem, recvown2_sem):
    group, path = lax.axis_index("group"), lax.axis_index("path")
    me = group * 16 + path
    loads = [pltpu.make_async_copy(a, b, load_sem.at[i]) for i, (a, b) in enumerate(
        [(outer_hbm, outer_ref), (mom_hbm, mom_ref), (route_hbm, route_ref), (owner_hbm, owner_ref)])]
    for load in loads:
        load.start()
    barrier = pltpu.get_barrier_semaphore()

    for s in route_order(n):
        pl.semaphore_signal(barrier, inc=1, device_id=peer(s, group, path), device_id_type=MESH)

    pl.semaphore_wait(barrier, n - 1)

    def exchange(*moves):
        for src, dst, _, recv in moves:
            pltpu.make_async_copy(src(me), dst(me), recv).start()

        for s in route_order(n):
            to = peer(s, group, path)
            rank = to[0] * 16 + to[1]
            for src, dst, sent, recv in moves:
                pltpu.make_async_remote_copy(
                    src(rank), dst(me), sent, recv, device_id=to, device_id_type=MESH).start()

    exchange((lambda r: x_ref.at[:, r, 0], lambda r: got_ref.at[0, r], send_sem.at[0], recv_sem.at[0]))
    for load in loads:
        load.wait()
    own_ref[...] = (1 - step) * outer_ref[...] - (outer_rate * momentum_decay * momentum_decay) * mom_ref[...]
    exchange((lambda r: own_ref.at[r], lambda r: gotown_ref.at[r], sendown_sem, recvown_sem))
    exchange((lambda r: x_ref.at[:, r, 1], lambda r: got_ref.at[1, r], send_sem.at[1], recv_sem.at[1]))

    rows = 4 * n
    route = route_ref[...].astype(f32).astype(bf16)
    k = lax.broadcasted_iota(jnp.int32, (2 * n, rows), 1) >> 1
    p = lax.broadcasted_iota(jnp.int32, (2 * n, rows), 0)
    both = jnp.dot(route, (k == p).astype(f32).astype(bf16), preferred_element_type=f32)
    level = lax.broadcasted_iota(jnp.int32, (1, rows), 1) & 1
    label = jnp.where(level == 0, both[0:1], both[1:2]).astype(jnp.int32) + 16 * level
    hot = (label == lax.broadcasted_iota(jnp.int32, (32, rows), 0)).astype(f32)
    counts = jnp.sum(hot, axis=1, keepdims=True)
    hot2 = jnp.concatenate([hot, hot], axis=0).T.astype(bf16)
    hot = hot.astype(bf16)
    r = lax.broadcasted_iota(jnp.int32, (32, 16), 0)
    owners = owner_ref[...]
    table = jnp.where(r < 16, owners[0:1], owners[1:2])
    mine = (r & 15) == lax.broadcasted_iota(jnp.int32, (32, 16), 1)
    owner_col = jnp.sum(jnp.where(mine, table, 0).astype(f32), axis=1, keepdims=True).astype(jnp.int32)
    own_hot = (owner_col == lax.broadcasted_iota(jnp.int32, (32, n), 1)).astype(f32)
    own_hot2 = jnp.concatenate([own_hot, own_hot], axis=0).T.astype(bf16)
    own_hot = own_hot.astype(bf16)
    owned = jnp.sum((owners == me).astype(f32)) > 0.5

    for t in range(2):
        pltpu.make_async_copy(got_ref.at[t], got_ref.at[t], recv_sem.at[t]).wait()
        if t == 0:
            pltpu.make_async_copy(gotown_ref, gotown_ref, recvown_sem).wait()
        mean = pick(hot, got_ref[t].reshape(rows, 128)) / counts
        fresh = step * mean + pick(own_hot, gotown_ref[:, t, :])
        res_ref[t] = spread(hot2, fresh).reshape(res_ref.shape[1:])
        resown_ref[:, t, :] = spread(own_hot2, mean)
        moves = [(lambda r: res_ref.at[t, r], lambda r: back_ref.at[:, r, t], send2_sem.at[t], recv2_sem.at[t])]
        if t == 1:
            moves.append((lambda r: resown_ref.at[r], lambda r: backown_ref.at[r], sendown2_sem, recvown2_sem))
        exchange(*moves)
    pltpu.make_async_copy(backown_ref, backown_ref, recvown2_sem).wait()
    delta = outer_ref[...] - backown_ref[...]
    newm_ref[...] = jnp.where(owned, momentum_decay * mom_ref[...] + delta, mom_ref[...])
    for t in range(2):
        pltpu.make_async_copy(got_ref.at[t], got_ref.at[t], recv2_sem.at[t]).wait()
    last = got_ref.at[0, pl.ds(0, n - 1)]
    for sem in (send_sem, send2_sem):
        for t in range(2):
            pltpu.make_async_copy(last, last, sem.at[t]).wait()
    lastown = gotown_ref.at[pl.ds(0, n - 1)]
    pltpu.make_async_copy(lastown, lastown, sendown_sem).wait()
    pltpu.make_async_copy(lastown, lastown, sendown2_sem).wait()


def settle(back_ref, newm_ref, out_ref, outm_ref, block_ref, row_ref, sems):
    size = back_ref.shape[1] // 2
    legs = [(newm_ref, row_ref, outm_ref)]
    for i in range(4):
        part = (i // 2, pl.ds(i % 2 * size, size))
        legs.append((back_ref.at[part], block_ref.at[part], out_ref.at[part]))
    loads = [pltpu.make_async_copy(a, b, sems.at[i]) for i, (a, b, _) in enumerate(legs)]
    stores = [pltpu.make_async_copy(b, c, sems.at[i]) for i, (_, b, c) in enumerate(legs)]
    for load in loads:
        load.start()
    for load, store in zip(loads, stores):
        load.wait()
        store.start()
    for store in stores:
        store.wait()


def on_device(inner_params, route, owner, outer_state, momentum):
    n = lax.axis_size(axes)
    x = inner_params.reshape(2, 2, n, 2, 128).transpose(0, 2, 3, 1, 4)
    vmem = pl.BlockSpec(memory_space=pltpu.VMEM)
    one = pltpu.SemaphoreType.DMA
    two = pltpu.SemaphoreType.DMA((2,))
    back, newm = pl.pallas_call(
        functools.partial(kernel, n),
        out_shape=(jax.ShapeDtypeStruct((2, n, 2, 2, 128), f32), jax.ShapeDtypeStruct((n, 2, 128), f32)),
        in_specs=[pl.BlockSpec(memory_space=pltpu.HBM)] * 5,
        out_specs=(pl.BlockSpec(memory_space=pltpu.HBM), vmem),
        scratch_shapes=[
            pltpu.VMEM((2, 2 * n), jnp.int32),
            pltpu.VMEM(owner.shape, jnp.int32),
            pltpu.VMEM((n, 2, 128), f32),
            pltpu.VMEM((n, 2, 128), f32),
            pltpu.SemaphoreType.DMA((4,)),
            pltpu.VMEM((n, 2, 128), f32),
            pltpu.VMEM((2, n, 2, 2, 128), f32),
            pltpu.VMEM((n, 2, 128), f32),
            pltpu.VMEM((2, n, 2, 2, 128), f32),
            pltpu.VMEM((n, 2, 128), f32),
            pltpu.VMEM((n, 2, 128), f32),
            two, two, one, one, two, two, one, one,
        ],
        compiler_params=pltpu.CompilerParams(collective_id=0, has_side_effects=True, vmem_limit_bytes=56 * 2**20),
    )(x, route.T, owner, outer_state.reshape(n, 2, 128), momentum.reshape(n, 2, 128))
    hbm = pl.BlockSpec(memory_space=pltpu.HBM)
    back, newm = pl.pallas_call(
        settle,
        out_shape=(jax.ShapeDtypeStruct(back.shape, f32), jax.ShapeDtypeStruct(newm.shape, f32)),
        in_specs=[hbm, hbm],
        out_specs=(hbm, hbm),
        scratch_shapes=[pltpu.VMEM(back.shape, f32), pltpu.VMEM(newm.shape, f32), pltpu.SemaphoreType.DMA((5,))],
        compiler_params=pltpu.CompilerParams(vmem_limit_bytes=56 * 2**20),
    )(back, newm)
    out = back.transpose(0, 3, 1, 2, 4).reshape(inner_params.shape)
    return out, newm.reshape(momentum.shape)


def solution(mesh):
    rows = P(axes, None)
    return jax.shard_map(
        on_device,
        mesh=mesh,
        in_specs=(P(axes, None, None), P(), P(), rows, rows),
        out_specs=(P(axes, None, None), rows),
        check_vma=False,
    )
```

```python
import functools

import jax
import jax.numpy as jnp
from jax import lax
from jax.experimental import pallas as pl
from jax.experimental.pallas import tpu as pltpu
from jax.sharding import PartitionSpec as P

axes = ("group", "path")
momentum_decay = 0.9
outer_rate = 0.7
step = outer_rate * (1 + momentum_decay)
MESH = pl.DeviceIdType.MESH
f32 = jnp.float32
bf16 = jnp.bfloat16


def split(x):
    high = x.astype(bf16)
    return high, (x - high.astype(f32)).astype(bf16)


def pick(hot, x):
    both = jnp.dot(hot, jnp.concatenate(split(x), axis=1), preferred_element_type=f32)
    return both[:, :128] + both[:, 128:]


def spread(hot2, x):
    return jnp.dot(hot2, jnp.concatenate(split(x), axis=0), preferred_element_type=f32)


def peer(s, group, path):
    core = ((group & 1) + (s >> 6)) & 1
    y = ((group >> 1) + ((s >> 4) & 3)) & 3
    z = ((path >> 2) + ((s >> 2) & 3)) & 3
    x = ((path & 3) + (s & 3)) & 3
    return y * 2 + core, z * 4 + x


def hops(s):
    return sum(min(a, 4 - a) for a in (s & 3, (s >> 2) & 3, (s >> 4) & 3))


def late_order():
    pairs = [(s, zz) for s in range(128) if not s & 12 for zz in range(4)]
    return sorted(pairs, key=lambda q: (-hops(q[0]) + q[1], q[0] * 37 % 128))


def route_order(n, whole=False):
    return sorted(range(0 if whole else 1, n), key=lambda s: (-hops(s), s * 37 % n))


def kernel(n, x_ref, route_hbm, owner_hbm, outer_hbm, mom_hbm, back_ref, newm_ref,
           route_ref, owner_ref, outer_ref, mom_ref, load_sem,
           own_ref, got_ref, gotown_ref, res_ref, resown_ref, backown_ref,
           send_sem, recv_sem, sendown_sem, recvown_sem, send2_sem, recv2_sem, sendown2_sem, recvown2_sem):
    group, path = lax.axis_index("group"), lax.axis_index("path")
    me = group * 16 + path
    loads = [pltpu.make_async_copy(a, b, load_sem.at[i]) for i, (a, b) in enumerate(
        [(outer_hbm, outer_ref), (mom_hbm, mom_ref), (route_hbm, route_ref), (owner_hbm, owner_ref)])]
    for load in loads:
        load.start()
    barrier = pltpu.get_barrier_semaphore()

    for s in route_order(n):
        pl.semaphore_signal(barrier, inc=1, device_id=peer(s, group, path), device_id_type=MESH)

    pl.semaphore_wait(barrier, n - 1)

    def exchange(*moves, late=False, cores=(0, 1), keep=True):
        for src, dst, _, recv in moves if keep else ():
            pltpu.make_async_copy(src(me), dst(me), recv).start()

        def post(to):
            rank = to[0] * 16 + to[1]
            for src, dst, sent, recv in moves:
                pltpu.make_async_remote_copy(
                    src(rank), dst(me), sent, recv, device_id=to, device_id_type=MESH).start()

        if late:
            z = path >> 2
            for d, zz in late_order():
                to = peer(d, group, path)
                to = (to[0], zz * 4 + (to[1] & 3))
                if d:
                    post(to)
                else:
                    pl.when(zz != z)(functools.partial(post, to))
        else:
            core = group & 1
            for cc in cores:
                for d in route_order(n // 2, True):
                    to = peer(d, group, path)
                    to = ((to[0] & 6) + cc, to[1])
                    if d:
                        post(to)
                    else:
                        pl.when(cc != core)(functools.partial(post, to))

    first = (lambda r: x_ref.at[:, r, 0], lambda r: got_ref.at[0, r], send_sem.at[0], recv_sem.at[0])
    own = (lambda r: own_ref.at[r], lambda r: gotown_ref.at[r], sendown_sem, recvown_sem)
    exchange(first, cores=(0,))
    for load in loads:
        load.wait()
    own_ref[...] = (1 - step) * outer_ref[...] - (outer_rate * momentum_decay * momentum_decay) * mom_ref[...]
    exchange(own, cores=(0,))
    exchange(first, cores=(1,), keep=False)
    exchange(own, cores=(1,), keep=False)
    exchange((lambda r: x_ref.at[:, r, 1], lambda r: got_ref.at[1, r], send_sem.at[1], recv_sem.at[1]))

    rows = 4 * n
    route = route_ref[...].astype(f32).astype(bf16)
    k = lax.broadcasted_iota(jnp.int32, (2 * n, rows), 1) >> 1
    p = lax.broadcasted_iota(jnp.int32, (2 * n, rows), 0)
    both = jnp.dot(route, (k == p).astype(f32).astype(bf16), preferred_element_type=f32)
    level = lax.broadcasted_iota(jnp.int32, (1, rows), 1) & 1
    label = jnp.where(level == 0, both[0:1], both[1:2]).astype(jnp.int32) + 16 * level
    hot = (label == lax.broadcasted_iota(jnp.int32, (32, rows), 0)).astype(f32)
    counts = jnp.sum(hot, axis=1, keepdims=True)
    hot2 = jnp.concatenate([hot, hot], axis=0).T.astype(bf16)
    hot = hot.astype(bf16)
    r = lax.broadcasted_iota(jnp.int32, (32, 16), 0)
    owners = owner_ref[...]
    table = jnp.where(r < 16, owners[0:1], owners[1:2])
    mine = (r & 15) == lax.broadcasted_iota(jnp.int32, (32, 16), 1)
    owner_col = jnp.sum(jnp.where(mine, table, 0).astype(f32), axis=1, keepdims=True).astype(jnp.int32)
    own_hot = (owner_col == lax.broadcasted_iota(jnp.int32, (32, n), 1)).astype(f32)
    own_hot2 = jnp.concatenate([own_hot, own_hot], axis=0).T.astype(bf16)
    own_hot = own_hot.astype(bf16)
    owned = jnp.sum((owners == me).astype(f32)) > 0.5

    for t in range(2):
        pltpu.make_async_copy(got_ref.at[t], got_ref.at[t], recv_sem.at[t]).wait()
        if t == 0:
            pltpu.make_async_copy(gotown_ref, gotown_ref, recvown_sem).wait()
        mean = pick(hot, got_ref[t].reshape(rows, 128)) / counts
        fresh = step * mean + pick(own_hot, gotown_ref[:, t, :])
        res_ref[t] = spread(hot2, fresh).reshape(res_ref.shape[1:])
        resown_ref[:, t, :] = spread(own_hot2, mean)
        moves = [(lambda r: res_ref.at[t, r], lambda r: back_ref.at[:, r, t], send2_sem.at[t], recv2_sem.at[t])]
        if t == 1:
            moves.append((lambda r: resown_ref.at[r], lambda r: backown_ref.at[r], sendown2_sem, recvown2_sem))
        exchange(*moves, late=True)
    pltpu.make_async_copy(backown_ref, backown_ref, recvown2_sem).wait()
    delta = outer_ref[...] - backown_ref[...]
    newm_ref[...] = jnp.where(owned, momentum_decay * mom_ref[...] + delta, mom_ref[...])
    for t in range(2):
        pltpu.make_async_copy(got_ref.at[t], got_ref.at[t], recv2_sem.at[t]).wait()
    last = got_ref.at[0, pl.ds(0, n - 1)]
    for sem in (send_sem, send2_sem):
        for t in range(2):
            pltpu.make_async_copy(last, last, sem.at[t]).wait()
    lastown = gotown_ref.at[pl.ds(0, n - 1)]
    pltpu.make_async_copy(lastown, lastown, sendown_sem).wait()
    pltpu.make_async_copy(lastown, lastown, sendown2_sem).wait()


def settle(back_ref, newm_ref, out_ref, outm_ref, block_ref, row_ref, sems):
    size = back_ref.shape[1] // 2
    legs = [(newm_ref, row_ref, outm_ref)]
    for i in range(4):
        part = (i // 2, pl.ds(i % 2 * size, size))
        legs.append((back_ref.at[part], block_ref.at[part], out_ref.at[part]))
    loads = [pltpu.make_async_copy(a, b, sems.at[i]) for i, (a, b, _) in enumerate(legs)]
    stores = [pltpu.make_async_copy(b, c, sems.at[i]) for i, (_, b, c) in enumerate(legs)]
    for load in loads:
        load.start()
    for load, store in zip(loads, stores):
        load.wait()
        store.start()
    for store in stores:
        store.wait()


def on_device(inner_params, route, owner, outer_state, momentum):
    n = lax.axis_size(axes)
    x = inner_params.reshape(2, 2, n, 2, 128).transpose(0, 2, 3, 1, 4)
    vmem = pl.BlockSpec(memory_space=pltpu.VMEM)
    one = pltpu.SemaphoreType.DMA
    two = pltpu.SemaphoreType.DMA((2,))
    back, newm = pl.pallas_call(
        functools.partial(kernel, n),
        out_shape=(jax.ShapeDtypeStruct((2, n, 2, 2, 128), f32), jax.ShapeDtypeStruct((n, 2, 128), f32)),
        in_specs=[pl.BlockSpec(memory_space=pltpu.HBM)] * 5,
        out_specs=(pl.BlockSpec(memory_space=pltpu.HBM), vmem),
        scratch_shapes=[
            pltpu.VMEM((2, 2 * n), jnp.int32),
            pltpu.VMEM(owner.shape, jnp.int32),
            pltpu.VMEM((n, 2, 128), f32),
            pltpu.VMEM((n, 2, 128), f32),
            pltpu.SemaphoreType.DMA((4,)),
            pltpu.VMEM((n, 2, 128), f32),
            pltpu.VMEM((2, n, 2, 2, 128), f32),
            pltpu.VMEM((n, 2, 128), f32),
            pltpu.VMEM((2, n, 2, 2, 128), f32),
            pltpu.VMEM((n, 2, 128), f32),
            pltpu.VMEM((n, 2, 128), f32),
            two, two, one, one, two, two, one, one,
        ],
        compiler_params=pltpu.CompilerParams(collective_id=0, has_side_effects=True, vmem_limit_bytes=56 * 2**20),
    )(x, route.T, owner, outer_state.reshape(n, 2, 128), momentum.reshape(n, 2, 128))
    hbm = pl.BlockSpec(memory_space=pltpu.HBM)
    back, newm = pl.pallas_call(
        settle,
        out_shape=(jax.ShapeDtypeStruct(back.shape, f32), jax.ShapeDtypeStruct(newm.shape, f32)),
        in_specs=[hbm, hbm],
        out_specs=(hbm, hbm),
        scratch_shapes=[pltpu.VMEM(back.shape, f32), pltpu.VMEM(newm.shape, f32), pltpu.SemaphoreType.DMA((5,))],
        compiler_params=pltpu.CompilerParams(vmem_limit_bytes=56 * 2**20),
    )(back, newm)
    out = back.transpose(0, 3, 1, 2, 4).reshape(inner_params.shape)
    return out, newm.reshape(momentum.shape)


def solution(mesh):
    rows = P(axes, None)
    return jax.shard_map(
        on_device,
        mesh=mesh,
        in_specs=(P(axes, None, None), P(), P(), rows, rows),
        out_specs=(P(axes, None, None), rows),
        check_vma=False,
    )
```

```python
import functools

import jax
import jax.numpy as jnp
from jax import lax
from jax.experimental import pallas as pl
from jax.experimental.pallas import tpu as pltpu
from jax.sharding import PartitionSpec as P

axes = ("group", "path")
momentum_decay = 0.9
outer_rate = 0.7
step = outer_rate * (1 + momentum_decay)
MESH = pl.DeviceIdType.MESH
f32 = jnp.float32
bf16 = jnp.bfloat16


def split(x):
    high = x.astype(bf16)
    return high, (x - high.astype(f32)).astype(bf16)


def pick(hot, x):
    both = jnp.dot(hot, jnp.concatenate(split(x), axis=1), preferred_element_type=f32)
    return both[:, :128] + both[:, 128:]


def spread(hot2, x):
    return jnp.dot(hot2, jnp.concatenate(split(x), axis=0), preferred_element_type=f32)


def peer(s, group, path):
    core = ((group & 1) + (s >> 6)) & 1
    y = ((group >> 1) + ((s >> 4) & 3)) & 3
    z = ((path >> 2) + ((s >> 2) & 3)) & 3
    x = ((path & 3) + (s & 3)) & 3
    return y * 2 + core, z * 4 + x


def hops(s):
    return sum(min(a, 4 - a) for a in (s & 3, (s >> 2) & 3, (s >> 4) & 3))


def late_order():
    spots = [(d, y, z) for d in (0, 1, 2, 3, 64, 65, 66, 67) for y in range(4) for z in range(4)]
    return sorted(spots, key=lambda q: ((0, 1, 2, 1)[q[1]] + (0, 2, 3, 2)[q[2]] - hops(q[0]), (q[0] * 37 + q[1] * 13 + q[2] * 7) % 31))


def route_order(n, whole=False):
    return sorted(range(0 if whole else 1, n), key=lambda s: (-hops(s), s * 37 % n))


def kernel(n, x_ref, route_hbm, owner_hbm, outer_hbm, mom_hbm, back_ref, newm_ref,
           route_ref, owner_ref, outer_ref, mom_ref, load_sem,
           own_ref, got_ref, gotown_ref, res_ref, resown_ref, backown_ref,
           send_sem, recv_sem, sendown_sem, recvown_sem, send2_sem, recv2_sem, sendown2_sem, recvown2_sem):
    group, path = lax.axis_index("group"), lax.axis_index("path")
    me = group * 16 + path
    loads = [pltpu.make_async_copy(a, b, load_sem.at[i]) for i, (a, b) in enumerate(
        [(outer_hbm, outer_ref), (mom_hbm, mom_ref), (route_hbm, route_ref), (owner_hbm, owner_ref)])]
    for load in loads:
        load.start()
    barrier = pltpu.get_barrier_semaphore()

    for s in route_order(n):
        pl.semaphore_signal(barrier, inc=1, device_id=peer(s, group, path), device_id_type=MESH)

    pl.semaphore_wait(barrier, n - 1)

    def exchange(*moves, late=False, cores=(1, 0), keep=True):
        for src, dst, _, recv in moves if keep else ():
            pltpu.make_async_copy(src(me), dst(me), recv).start()

        def post(to):
            rank = to[0] * 16 + to[1]
            for src, dst, sent, recv in moves:
                pltpu.make_async_remote_copy(
                    src(rank), dst(me), sent, recv, device_id=to, device_id_type=MESH).start()

        if late:
            for d, y, z in late_order():
                to = peer(d, group, path)
                to = (y * 2 + (to[0] & 1), z * 4 + (to[1] & 3))
                if d:
                    post(to)
                else:
                    away = jnp.logical_or(y != group >> 1, z != path >> 2)
                    pl.when(away)(functools.partial(post, to))
        else:
            core = group & 1
            for cc in cores:
                for d in route_order(n // 2, True):
                    to = peer(d, group, path)
                    to = ((to[0] & 6) + cc, to[1])
                    if d:
                        post(to)
                    else:
                        pl.when(cc != core)(functools.partial(post, to))

    first = (lambda r: x_ref.at[:, r, 0], lambda r: got_ref.at[0, r], send_sem.at[0], recv_sem.at[0])
    own = (lambda r: own_ref.at[0, r], lambda r: gotown_ref.at[0, r], sendown_sem.at[0], recvown_sem.at[0])
    own1 = (lambda r: own_ref.at[1, r], lambda r: gotown_ref.at[1, r], sendown_sem.at[1], recvown_sem.at[1])
    exchange(first, cores=(1,))
    for load in loads:
        load.wait()
    for t in range(2):
        own_row = (1 - step) * outer_ref[:, t, :] - (outer_rate * momentum_decay * momentum_decay) * mom_ref[:, t, :]
        own_ref[t] = own_row.reshape(n, 1, 128)
    exchange(own, cores=(1,))
    exchange(first, own, cores=(0,), keep=False)
    exchange((lambda r: x_ref.at[:, r, 1], lambda r: got_ref.at[1, r], send_sem.at[1], recv_sem.at[1]), own1)

    rows = 4 * n
    route = route_ref[...].astype(f32).astype(bf16)
    k = lax.broadcasted_iota(jnp.int32, (2 * n, rows), 1) >> 1
    p = lax.broadcasted_iota(jnp.int32, (2 * n, rows), 0)
    both = jnp.dot(route, (k == p).astype(f32).astype(bf16), preferred_element_type=f32)
    level = lax.broadcasted_iota(jnp.int32, (1, rows), 1) & 1
    label = jnp.where(level == 0, both[0:1], both[1:2]).astype(jnp.int32) + 16 * level
    hot = (label == lax.broadcasted_iota(jnp.int32, (32, rows), 0)).astype(f32)
    counts = jnp.sum(hot, axis=1, keepdims=True)
    hot2 = jnp.concatenate([hot, hot], axis=0).T.astype(bf16)
    hot = hot.astype(bf16)
    r = lax.broadcasted_iota(jnp.int32, (32, 16), 0)
    owners = owner_ref[...]
    table = jnp.where(r < 16, owners[0:1], owners[1:2])
    mine = (r & 15) == lax.broadcasted_iota(jnp.int32, (32, 16), 1)
    owner_col = jnp.sum(jnp.where(mine, table, 0).astype(f32), axis=1, keepdims=True).astype(jnp.int32)
    own_hot = (owner_col == lax.broadcasted_iota(jnp.int32, (32, n), 1)).astype(f32)
    own_hot2 = jnp.concatenate([own_hot, own_hot], axis=0).T.astype(bf16)
    own_hot = own_hot.astype(bf16)
    owned = jnp.sum((owners == me).astype(f32)) > 0.5

    for t in range(2):
        pltpu.make_async_copy(got_ref.at[t], got_ref.at[t], recv_sem.at[t]).wait()
        pltpu.make_async_copy(gotown_ref.at[t], gotown_ref.at[t], recvown_sem.at[t]).wait()
        mean = pick(hot, got_ref[t].reshape(rows, 128)) / counts
        fresh = step * mean + pick(own_hot, gotown_ref[t].reshape(n, 128))
        res_ref[t] = spread(hot2, fresh).reshape(res_ref.shape[1:])
        resown_ref[:, t, :] = spread(own_hot2, mean)
        moves = [(lambda r: res_ref.at[t, r], lambda r: back_ref.at[:, r, t], send2_sem.at[t], recv2_sem.at[t])]
        if t == 1:
            moves.append((lambda r: resown_ref.at[r], lambda r: backown_ref.at[r], sendown2_sem, recvown2_sem))
        exchange(*moves, late=True)
    last = got_ref.at[0, pl.ds(0, n - 1)]
    for t in range(2):
        pltpu.make_async_copy(last, last, send_sem.at[t]).wait()
    for t in range(2):
        lastown = gotown_ref.at[t, pl.ds(0, n - 1)]
        pltpu.make_async_copy(lastown, lastown, sendown_sem.at[t]).wait()
    lastown = backown_ref.at[pl.ds(0, n - 1)]
    pltpu.make_async_copy(backown_ref, backown_ref, recvown2_sem).wait()
    delta = outer_ref[...] - backown_ref[...]
    mom_ref[...] = jnp.where(owned, momentum_decay * mom_ref[...] + delta, mom_ref[...])
    store = pltpu.make_async_copy(mom_ref, newm_ref, load_sem.at[1])
    store.start()
    for t in range(2):
        pltpu.make_async_copy(got_ref.at[t], got_ref.at[t], recv2_sem.at[t]).wait()
    for t in range(2):
        pltpu.make_async_copy(last, last, send2_sem.at[t]).wait()
    pltpu.make_async_copy(lastown, lastown, sendown2_sem).wait()
    store.wait()


def settle(back_ref, newm_ref, out_ref, outm_ref, block_ref, row_ref, sems):
    size = back_ref.shape[1] // 2
    legs = [(newm_ref, row_ref, outm_ref)]
    for i in range(4):
        part = (i // 2, pl.ds(i % 2 * size, size))
        legs.append((back_ref.at[part], block_ref.at[part], out_ref.at[part]))
    loads = [pltpu.make_async_copy(a, b, sems.at[i]) for i, (a, b, _) in enumerate(legs)]
    stores = [pltpu.make_async_copy(b, c, sems.at[i]) for i, (_, b, c) in enumerate(legs)]
    for load in loads:
        load.start()
    for load, store in zip(loads, stores):
        load.wait()
        store.start()
    for store in stores:
        store.wait()


def on_device(inner_params, route, owner, outer_state, momentum):
    n = lax.axis_size(axes)
    x = inner_params.reshape(2, 2, n, 2, 128).transpose(0, 2, 3, 1, 4)
    vmem = pl.BlockSpec(memory_space=pltpu.VMEM)
    one = pltpu.SemaphoreType.DMA
    two = pltpu.SemaphoreType.DMA((2,))
    back, newm = pl.pallas_call(
        functools.partial(kernel, n),
        out_shape=(jax.ShapeDtypeStruct((2, n, 2, 2, 128), f32), jax.ShapeDtypeStruct((n, 2, 128), f32)),
        in_specs=[pl.BlockSpec(memory_space=pltpu.HBM)] * 5,
        out_specs=(pl.BlockSpec(memory_space=pltpu.HBM), pl.BlockSpec(memory_space=pltpu.HBM)),
        scratch_shapes=[
            pltpu.VMEM((2, 2 * n), jnp.int32),
            pltpu.VMEM(owner.shape, jnp.int32),
            pltpu.VMEM((n, 2, 128), f32),
            pltpu.VMEM((n, 2, 128), f32),
            pltpu.SemaphoreType.DMA((4,)),
            pltpu.VMEM((2, n, 1, 128), f32),
            pltpu.VMEM((2, n, 2, 2, 128), f32),
            pltpu.VMEM((2, n, 1, 128), f32),
            pltpu.VMEM((2, n, 2, 2, 128), f32),
            pltpu.VMEM((n, 2, 128), f32),
            pltpu.VMEM((n, 2, 128), f32),
            two, two, two, two, two, two, one, one,
        ],
        compiler_params=pltpu.CompilerParams(collective_id=0, has_side_effects=True, vmem_limit_bytes=56 * 2**20),
    )(x, route.T, owner, outer_state.reshape(n, 2, 128), momentum.reshape(n, 2, 128))
    hbm = pl.BlockSpec(memory_space=pltpu.HBM)
    back, newm = pl.pallas_call(
        settle,
        out_shape=(jax.ShapeDtypeStruct(back.shape, f32), jax.ShapeDtypeStruct(newm.shape, f32)),
        in_specs=[hbm, hbm],
        out_specs=(hbm, hbm),
        scratch_shapes=[pltpu.VMEM(back.shape, f32), pltpu.VMEM(newm.shape, f32), pltpu.SemaphoreType.DMA((5,))],
        compiler_params=pltpu.CompilerParams(vmem_limit_bytes=56 * 2**20),
    )(back, newm)
    out = back.transpose(0, 3, 1, 2, 4).reshape(inner_params.shape)
    return out, newm.reshape(momentum.shape)


def solution(mesh):
    rows = P(axes, None)
    return jax.shard_map(
        on_device,
        mesh=mesh,
        in_specs=(P(axes, None, None), P(), P(), rows, rows),
        out_specs=(P(axes, None, None), rows),
        check_vma=False,
    )
```

```python
import functools

import jax
import jax.numpy as jnp
from jax import lax
from jax.experimental import pallas as pl
from jax.experimental.pallas import tpu as pltpu
from jax.sharding import PartitionSpec as P

axes = ("group", "path")
momentum_decay = 0.9
outer_rate = 0.7
step = outer_rate * (1 + momentum_decay)
MESH = pl.DeviceIdType.MESH
f32 = jnp.float32
bf16 = jnp.bfloat16


def split(x):
    high = x.astype(bf16)
    return high, (x - high.astype(f32)).astype(bf16)


def pick(hot, x):
    both = jnp.dot(hot, jnp.concatenate(split(x), axis=1), preferred_element_type=f32)
    return both[:, :128] + both[:, 128:]


def spread(hot2, x):
    return jnp.dot(hot2, jnp.concatenate(split(x), axis=0), preferred_element_type=f32)


def peer(s, group, path):
    core = ((group & 1) + (s >> 6)) & 1
    y = ((group >> 1) + ((s >> 4) & 3)) & 3
    z = ((path >> 2) + ((s >> 2) & 3)) & 3
    x = ((path & 3) + (s & 3)) & 3
    return y * 2 + core, z * 4 + x


def hops(s):
    return sum(min(a, 4 - a) for a in (s & 3, (s >> 2) & 3, (s >> 4) & 3))


def late_order():
    spots = [(d, y, z) for d in (0, 1, 2, 3, 64, 65, 66, 67) for y in range(4) for z in range(4)]
    return sorted(spots, key=lambda q: ((0, 1, 2, 1)[q[1]] + (0, 2, 4, 4)[q[2]] - hops(q[0]) - (q[0] > 63), (q[0] * 37 + q[1] * 13 + q[2] * 7) % 31))


def route_order(n, whole=False):
    return sorted(range(0 if whole else 1, n), key=lambda s: (-hops(s), s * 37 % n))


def kernel(n, x_ref, route_hbm, owner_hbm, outer_hbm, mom_hbm, back_ref, newm_ref,
           route_ref, owner_ref, outer_ref, mom_ref, load_sem,
           own_ref, got_ref, gotown_ref, res_ref, resown_ref, backown_ref,
           send_sem, recv_sem, sendown_sem, recvown_sem, send2_sem, recv2_sem, sendown2_sem, recvown2_sem):
    group, path = lax.axis_index("group"), lax.axis_index("path")
    me = group * 16 + path
    loads = [pltpu.make_async_copy(a, b, load_sem.at[i]) for i, (a, b) in enumerate(
        [(outer_hbm, outer_ref), (mom_hbm, mom_ref), (route_hbm, route_ref), (owner_hbm, owner_ref)])]
    for load in loads:
        load.start()
    barrier = pltpu.get_barrier_semaphore()

    for s in route_order(n):
        pl.semaphore_signal(barrier, inc=1, device_id=peer(s, group, path), device_id_type=MESH)

    pl.semaphore_wait(barrier, n - 1)

    def exchange(*moves, late=False, cores=(1, 0), keep=True):
        for src, dst, _, recv in moves if keep else ():
            pltpu.make_async_copy(src(me), dst(me), recv).start()

        def post(to):
            rank = to[0] * 16 + to[1]
            for src, dst, sent, recv in moves:
                pltpu.make_async_remote_copy(
                    src(rank), dst(me), sent, recv, device_id=to, device_id_type=MESH).start()

        if late:
            for d, y, z in late_order():
                to = peer(d, group, path)
                to = (y * 2 + (to[0] & 1), z * 4 + (to[1] & 3))
                if d:
                    post(to)
                else:
                    away = jnp.logical_or(y != group >> 1, z != path >> 2)
                    pl.when(away)(functools.partial(post, to))
        else:
            core = group & 1
            for cc in cores:
                for d in route_order(n // 2, True):
                    to = peer(d, group, path)
                    to = ((to[0] & 6) + cc, to[1])
                    if d:
                        post(to)
                    else:
                        pl.when(cc != core)(functools.partial(post, to))

    first = (lambda r: x_ref.at[:, r, 0], lambda r: got_ref.at[0, r], send_sem.at[0], recv_sem.at[0])
    own = (lambda r: own_ref.at[0, r], lambda r: gotown_ref.at[0, r], sendown_sem.at[0], recvown_sem.at[0])
    own1 = (lambda r: own_ref.at[1, r], lambda r: gotown_ref.at[1, r], sendown_sem.at[1], recvown_sem.at[1])
    exchange(first, cores=(1,))
    for load in loads:
        load.wait()
    for t in range(2):
        own_row = (1 - step) * outer_ref[:, t, :] - (outer_rate * momentum_decay * momentum_decay) * mom_ref[:, t, :]
        own_ref[t] = own_row.reshape(n, 1, 128)
    exchange(own, cores=(1,))
    exchange(first, own, cores=(0,), keep=False)
    exchange((lambda r: x_ref.at[:, r, 1], lambda r: got_ref.at[1, r], send_sem.at[1], recv_sem.at[1]), own1)

    rows = 4 * n
    route = route_ref[...].astype(f32).astype(bf16)
    k = lax.broadcasted_iota(jnp.int32, (2 * n, rows), 1) >> 1
    p = lax.broadcasted_iota(jnp.int32, (2 * n, rows), 0)
    both = jnp.dot(route, (k == p).astype(f32).astype(bf16), preferred_element_type=f32)
    level = lax.broadcasted_iota(jnp.int32, (1, rows), 1) & 1
    label = jnp.where(level == 0, both[0:1], both[1:2]).astype(jnp.int32) + 16 * level
    hot = (label == lax.broadcasted_iota(jnp.int32, (32, rows), 0)).astype(f32)
    counts = jnp.sum(hot, axis=1, keepdims=True)
    hot2 = jnp.concatenate([hot, hot], axis=0).T.astype(bf16)
    hot = hot.astype(bf16)
    r = lax.broadcasted_iota(jnp.int32, (32, 16), 0)
    owners = owner_ref[...]
    table = jnp.where(r < 16, owners[0:1], owners[1:2])
    mine = (r & 15) == lax.broadcasted_iota(jnp.int32, (32, 16), 1)
    owner_col = jnp.sum(jnp.where(mine, table, 0).astype(f32), axis=1, keepdims=True).astype(jnp.int32)
    own_hot = (owner_col == lax.broadcasted_iota(jnp.int32, (32, n), 1)).astype(f32)
    own_hot2 = jnp.concatenate([own_hot, own_hot], axis=0).T.astype(bf16)
    own_hot = own_hot.astype(bf16)
    owned = jnp.sum((owners == me).astype(f32)) > 0.5

    for t in range(2):
        pltpu.make_async_copy(got_ref.at[t], got_ref.at[t], recv_sem.at[t]).wait()
        pltpu.make_async_copy(gotown_ref.at[t], gotown_ref.at[t], recvown_sem.at[t]).wait()
        mean = pick(hot, got_ref[t].reshape(rows, 128)) / counts
        fresh = step * mean + pick(own_hot, gotown_ref[t].reshape(n, 128))
        resown_ref[t] = spread(own_hot2, mean).reshape(resown_ref.shape[1:])
        res_ref[t] = spread(hot2, fresh).reshape(res_ref.shape[1:])
        exchange((lambda r: res_ref.at[t, r], lambda r: back_ref.at[:, r, t], send2_sem.at[t], recv2_sem.at[t]),
                 (lambda r: resown_ref.at[t, r], lambda r: backown_ref.at[t, r], sendown2_sem.at[t], recvown2_sem.at[t]),
                 late=True)
    last = got_ref.at[0, pl.ds(0, n - 1)]
    for t in range(2):
        pltpu.make_async_copy(last, last, send_sem.at[t]).wait()
    for t in range(2):
        lastown = gotown_ref.at[t, pl.ds(0, n - 1)]
        pltpu.make_async_copy(lastown, lastown, sendown_sem.at[t]).wait()
    for t in range(2):
        pltpu.make_async_copy(backown_ref.at[t], backown_ref.at[t], recvown2_sem.at[t]).wait()
        held = mom_ref[:, t, :]
        delta = outer_ref[:, t, :] - backown_ref[t].reshape(n, 128)
        mom_ref[:, t, :] = jnp.where(owned, momentum_decay * held + delta, held)
    store = pltpu.make_async_copy(mom_ref, newm_ref, load_sem.at[1])
    store.start()
    for t in range(2):
        pltpu.make_async_copy(got_ref.at[t], got_ref.at[t], recv2_sem.at[t]).wait()
    for t in range(2):
        pltpu.make_async_copy(last, last, send2_sem.at[t]).wait()
    for t in range(2):
        lastown = backown_ref.at[t, pl.ds(0, n - 1)]
        pltpu.make_async_copy(lastown, lastown, sendown2_sem.at[t]).wait()
    store.wait()


def settle(back_ref, newm_ref, out_ref, outm_ref, block_ref, row_ref, sems):
    size = back_ref.shape[1] // 2
    legs = [(newm_ref, row_ref, outm_ref)]
    for i in range(4):
        part = (i // 2, pl.ds(i % 2 * size, size))
        legs.append((back_ref.at[part], block_ref.at[part], out_ref.at[part]))
    loads = [pltpu.make_async_copy(a, b, sems.at[i]) for i, (a, b, _) in enumerate(legs)]
    stores = [pltpu.make_async_copy(b, c, sems.at[i]) for i, (_, b, c) in enumerate(legs)]
    for load in loads:
        load.start()
    for load, store in zip(loads, stores):
        load.wait()
        store.start()
    for store in stores:
        store.wait()


def on_device(inner_params, route, owner, outer_state, momentum):
    n = lax.axis_size(axes)
    x = inner_params.reshape(2, 2, n, 2, 128).transpose(0, 2, 3, 1, 4)
    vmem = pl.BlockSpec(memory_space=pltpu.VMEM)
    one = pltpu.SemaphoreType.DMA
    two = pltpu.SemaphoreType.DMA((2,))
    back, newm = pl.pallas_call(
        functools.partial(kernel, n),
        out_shape=(jax.ShapeDtypeStruct((2, n, 2, 2, 128), f32), jax.ShapeDtypeStruct((n, 2, 128), f32)),
        in_specs=[pl.BlockSpec(memory_space=pltpu.HBM)] * 5,
        out_specs=(pl.BlockSpec(memory_space=pltpu.HBM), pl.BlockSpec(memory_space=pltpu.HBM)),
        scratch_shapes=[
            pltpu.VMEM((2, 2 * n), jnp.int32),
            pltpu.VMEM(owner.shape, jnp.int32),
            pltpu.VMEM((n, 2, 128), f32),
            pltpu.VMEM((n, 2, 128), f32),
            pltpu.SemaphoreType.DMA((4,)),
            pltpu.VMEM((2, n, 1, 128), f32),
            pltpu.VMEM((2, n, 2, 2, 128), f32),
            pltpu.VMEM((2, n, 1, 128), f32),
            pltpu.VMEM((2, n, 2, 2, 128), f32),
            pltpu.VMEM((2, n, 1, 128), f32),
            pltpu.VMEM((2, n, 1, 128), f32),
            two, two, two, two, two, two, two, two,
        ],
        compiler_params=pltpu.CompilerParams(collective_id=0, has_side_effects=True, vmem_limit_bytes=56 * 2**20),
    )(x, route.T, owner, outer_state.reshape(n, 2, 128), momentum.reshape(n, 2, 128))
    hbm = pl.BlockSpec(memory_space=pltpu.HBM)
    back, newm = pl.pallas_call(
        settle,
        out_shape=(jax.ShapeDtypeStruct(back.shape, f32), jax.ShapeDtypeStruct(newm.shape, f32)),
        in_specs=[hbm, hbm],
        out_specs=(hbm, hbm),
        scratch_shapes=[pltpu.VMEM(back.shape, f32), pltpu.VMEM(newm.shape, f32), pltpu.SemaphoreType.DMA((5,))],
        compiler_params=pltpu.CompilerParams(vmem_limit_bytes=56 * 2**20),
    )(back, newm)
    out = back.transpose(0, 3, 1, 2, 4).reshape(inner_params.shape)
    return out, newm.reshape(momentum.shape)


def solution(mesh):
    rows = P(axes, None)
    return jax.shard_map(
        on_device,
        mesh=mesh,
        in_specs=(P(axes, None, None), P(), P(), rows, rows),
        out_specs=(P(axes, None, None), rows),
        check_vma=False,
    )
```
